256 devices in a mesh: row: 8 (over y, core), col: 32 (over x, z).
Axes of the slice: x: 4, y: 4, z: 8, core: 2. Of those that a mesh axis runs over, the one named last changes fastest.
Arguments:
- quant_acts: bfloat16 [4096, 8192], P('col', 'row'), may hold values from -6 to 6
- full_acts: bfloat16 [4096, 8192], P('col', 'row'), may hold values from -6 to 6
Outputs:
- hessian: float32 [8192, 8192], P('row', 'col')
- cross_term: float32 [8192, 8192], P('row', 'col')
The draws below stay inside these ranges and needn't reach their ends.
All inputs are finite; a program needn't handle non-finite values.
Results may differ from the reference program's by a relative error of at most 0.0028.
Values may be sent and summed in bfloat16 or wider, within the bound.
A program may use at most 64 MiB of HBM per device.

```python
import jax
import jax.numpy as jnp

SLAB = 8192
TOKENS = 4096


def level_of(key, shape, pieces, low, top_value):
    def one(position, blocks):
        heights = jax.random.uniform(jax.random.fold_in(jax.random.fold_in(key, 6), position), (blocks,), jnp.float32, low / len(pieces), top_value / len(pieces))
        return jnp.repeat(jnp.exp(heights), shape[position] // blocks).reshape((-1,) + (1,) * (len(shape) - position - 1))

    gain = one(*pieces[0])
    for cut in pieces[1:]:
        gain = gain * one(*cut)
    return gain


def scatter_about(key, shape, scale, bound, split=(), dtype=jnp.bfloat16):
    factor_of = level_of(key, shape, split, -0.22, 0.18) if split else 1.0
    result = jax.random.normal(key, shape, jnp.float32) * scale * factor_of
    return jnp.minimum(jnp.maximum(result, -bound), bound).astype(dtype)


def setup_inputs(seed: int = 0) -> dict:
    splits = jax.random.split(jax.random.key(seed), 3)
    quant_acts = scatter_about(splits[0], (TOKENS, SLAB), 1.0, 6.0, ((0, 32), (1, 8)))
    full_acts = scatter_about(splits[1], (TOKENS, SLAB), 1.0, 6.0, ((0, 32), (1, 8)))
    return {"quant_acts": quant_acts, "full_acts": full_acts}


def reference(quant_acts, full_acts):
    deltas = (full_acts.astype(jnp.float32) - quant_acts.astype(jnp.float32)).astype(jnp.bfloat16)
    scale = 1.0 / TOKENS
    hessian = jnp.dot(quant_acts.T, quant_acts, preferred_element_type=jnp.float32) * scale
    cross_term = jnp.dot(deltas.T, quant_acts, preferred_element_type=jnp.float32) * scale
    return hessian, cross_term
```

```python
import jax
import jax.numpy as jnp
from jax import lax
from jax.experimental import pallas as pl
from jax.experimental.pallas import tpu as pltpu
from jax.sharding import PartitionSpec as P

MESH = pl.DeviceIdType.MESH
NX, NY, NZ = 4, 4, 8
TOK, FEAT, SUB = 128, 1024, 256
CH = 128
NQ = FEAT // CH
NJ = 2 * NQ
HALF = CH // 2
ORDER = (1, 7, 2, 6, 3, 5, 4)


def wrap(v, n):
    return lax.rem(v + n, n)


def kernel(q_ref, f_ref, o_ref, rows, cols, part, s1, r1, s2, r2,
           zsend, zrecv, asend, arecv, ysend, yrecv, ksend, krecv, xsend, xrecv):
    r, c = lax.axis_index("row"), lax.axis_index("col")
    y, k = lax.div(r, 2), lax.rem(r, 2)
    x, z = lax.div(c, NZ), lax.rem(c, NZ)
    xr, xl, xo = wrap(x + 1, NX), wrap(x - 1, NX), wrap(x + 2, NX)
    yr, yl, yo = wrap(y + 1, NY), wrap(y - 1, NY), wrap(y + 2, NY)
    zr, zl = wrap(z + 1, NZ), wrap(z - 1, NZ)
    owner = lax.div(z, 4) == k

    def dev(x, y, z, k):
        return (y * 2 + k, x * NZ + z)

    right, left = dev(x, y, zr, k), dev(x, y, zl, k)
    xright, xleft = dev(xr, y, z, k), dev(xl, y, z, k)
    up, down = dev(x, yr, z, k), dev(x, yl, z, k)
    other = dev(x, y, z, 1 - k)

    def remote(src, dst, send, recv, to):
        return pltpu.make_async_remote_copy(
            src_ref=src, dst_ref=dst, send_sem=send, recv_sem=recv, device_id=to, device_id_type=MESH
        )

    barrier = pltpu.get_barrier_semaphore()
    for d in range(1, NZ):
        pl.semaphore_signal(barrier, inc=1, device_id=dev(x, y, wrap(z + d, NZ), k), device_id_type=MESH)
    for to in (xright, xleft, up, down, other):
        pl.semaphore_signal(barrier, inc=1, device_id=to, device_id_type=MESH)

    for j in range(NQ):
        qj = q_ref[:, j * CH : (j + 1) * CH].astype(jnp.float32)
        fj = f_ref[:, j * CH : (j + 1) * CH].astype(jnp.float32)
        rows[j, z] = qj.T.astype(jnp.bfloat16)
        rows[NQ + j, z] = (fj - qj).astype(jnp.bfloat16).astype(jnp.float32).T.astype(jnp.bfloat16)

    pl.semaphore_wait(barrier, NZ - 1 + 5)

    def zcopy(j, s, way):
        at = wrap(z - s, NZ) if way == 0 else lax.rem(z + s, NZ)
        ref = rows.at[j, at]
        if s == 3:
            ref = rows.at[j, at, pl.ds(way * HALF, HALF)]
        return remote(ref, ref, zsend.at[j, s, way], zrecv.at[j, s, way], (right, left)[way])

    def zarrived(j, s, way):
        at = wrap(z - s - 1, NZ) if way == 0 else lax.rem(z + s + 1, NZ)
        ref = rows.at[j, at]
        if s == 3:
            ref = rows.at[j, at, pl.ds(way * HALF, HALF)]
        remote(ref, ref, zsend.at[j, s, way], zrecv.at[j, s, way], (right, left)[way]).wait_recv()

    def zslot(t, guard=True):
        for s in range(4):
            j = t - s

            def go(j=j, s=s):
                for way in range(2):
                    if s > 0:
                        zarrived(j, s - 1, way)
                    zcopy(j, s, way).start()

            if guard:
                pl.when(jnp.logical_and(j >= 0, j < NJ))(go)
            elif j >= 0:
                go()

    def acopy(d):
        to = wrap(z + d, NZ)
        src = q_ref.at[:, pl.ds(pl.multiple_of(lax.rem(to, 4) * SUB, SUB), SUB)]
        return remote(src, cols.at[y, z], asend.at[d - 1], arecv.at[d - 1], dev(x, y, to, k))

    for d in ORDER:
        pl.when(lax.div(wrap(z + d, NZ), 4) == k)(lambda d=d: acopy(d).start())

    zslot(0, False)

    @pl.when(owner)
    def _():
        cols[y, z] = q_ref[:, pl.ds(pl.multiple_of(lax.rem(z, 4) * SUB, SUB), SUB)]

    zslot(1, False)

    def ycopy(b, i, s, way):
        if s == 0:
            ref = cols.at[y, b]
        else:
            ref = cols.at[(yl, yr)[way], b, pl.ds(way * 64, 64)]
        return remote(ref, ref, ysend.at[i, s, way], yrecv.at[i, s, way], (up, down)[way])

    def yarrived(b, i, s, way):
        if s == 0:
            ref = cols.at[(yl, yr)[way], b]
        else:
            ref = cols.at[yo, b, pl.ds(way * 64, 64)]
        remote(ref, ref, ysend.at[i, s, way], yrecv.at[i, s, way], (up, down)[way]).wait_recv()

    def kcopy(yb, b, i, n):
        ref = cols.at[yb, b]
        return remote(ref, ref, ksend.at[i, n], krecv.at[i, n], other)

    SRC = (0,) + ORDER

    @pl.when(owner)
    def _():
        for i, d in enumerate(SRC):
            b = wrap(z - d, NZ)
            if d:
                remote(cols.at[y, b], cols.at[y, b], asend.at[d - 1], arecv.at[d - 1], other).wait_recv()
            ycopy(b, i, 0, 0).start()
            ycopy(b, i, 0, 1).start()
            kcopy(y, b, i, 0).start()

    zslot(2, False)

    @pl.when(owner)
    def _():
        for i, d in enumerate(SRC):
            b = wrap(z - d, NZ)
            for way in range(2):
                yarrived(b, i, 0, way)
                ycopy(b, i, 1, way).start()
                kcopy((yl, yr)[way], b, i, 1 + way).start()

    zslot(3, False)

    @pl.when(owner)
    def _():
        for i, d in enumerate(SRC):
            b = wrap(z - d, NZ)
            for way in range(2):
                yarrived(b, i, 1, way)
            kcopy(yo, b, i, 3).start()

    @pl.when(jnp.logical_not(owner))
    def _():
        for i, d in enumerate(SRC):
            b = wrap(z - d, NZ)
            for n, yb in enumerate((y, yl, yr, yo)):
                kcopy(yb, b, i, n).wait_recv()

    def x1copy(j, way):
        return remote(s1.at[j, way], r1.at[j, way], xsend.at[j, 0, way], xrecv.at[j, 0, way], (xright, xleft)[way])

    def x2copy(j, way):
        return remote(s2.at[j, way], r2.at[j, way], xsend.at[j, 1, way], xrecv.at[j, 1, way], (xright, xleft)[way])

    def product(j):
        for way in range(2):
            zarrived(j, 3, way)
        a = jnp.concatenate([rows[j, b] for b in range(NZ)], axis=1)

        def times(dest):
            b = cols[dest].reshape(NZ * TOK, SUB)
            return jnp.dot(a, b, preferred_element_type=jnp.float32)

        far = times(xo).astype(jnp.bfloat16)
        s1[j, 0] = far[:HALF]
        s1[j, 1] = far[HALF:]
        x1copy(j, 0).start()
        x1copy(j, 1).start()
        slot = lax.rem(j, 4)
        part[slot, 0] = times(xr)
        part[slot, 1] = times(xl)
        part[slot, 2] = times(x)

    def pass_on(j):
        slot = lax.rem(j, 4)
        x1copy(j, 0).wait_recv()
        s2[j, 0, :HALF] = (part[slot, 0, :HALF] + r1[j, 0].astype(jnp.float32)).astype(jnp.bfloat16)
        s2[j, 0, HALF:] = part[slot, 0, HALF:].astype(jnp.bfloat16)
        x2copy(j, 0).start()
        x1copy(j, 1).wait_recv()
        s2[j, 1, HALF:] = (part[slot, 1, HALF:] + r1[j, 1].astype(jnp.float32)).astype(jnp.bfloat16)
        s2[j, 1, :HALF] = part[slot, 1, :HALF].astype(jnp.bfloat16)
        x2copy(j, 1).start()

    def finish(j):
        slot = lax.rem(j, 4)
        x2copy(j, 0).wait_recv()
        x2copy(j, 1).wait_recv()
        total = part[slot, 2] + r2[j, 0].astype(jnp.float32) + r2[j, 1].astype(jnp.float32)
        o_ref[pl.ds(pl.multiple_of(j * CH, CH), CH), :] = total

    def slot(t, carry):
        zslot(t)
        for lag, work in ((4, product), (5, pass_on), (6, finish)):
            j = t - lag
            pl.when(jnp.logical_and(j >= 0, j < NJ))(lambda j=j, work=work: work(j))
        return carry

    lax.fori_loop(4, NJ + 6, slot, 0)

    def drain(j, carry):
        for way in range(2):
            for s in range(4):
                zcopy(j, s, way).wait_send()
            x1copy(j, way).wait_send()
            x2copy(j, way).wait_send()
        return carry

    lax.fori_loop(0, NJ, drain, 0)
    for d in ORDER:
        pl.when(lax.div(wrap(z + d, NZ), 4) == k)(lambda d=d: acopy(d).wait_send())

    @pl.when(owner)
    def _():
        for i, d in enumerate(SRC):
            b = wrap(z - d, NZ)
            for way in range(2):
                ycopy(b, i, 0, way).wait_send()
                ycopy(b, i, 1, way).wait_send()
            for n, yb in enumerate((y, yl, yr, yo)):
                kcopy(yb, b, i, n).wait_send()


def local(quant_acts, full_acts):
    bf16, f32, dma = jnp.bfloat16, jnp.float32, pltpu.SemaphoreType.DMA
    out = pl.pallas_call(
        kernel,
        out_shape=jax.ShapeDtypeStruct((2 * FEAT, SUB), f32),
        in_specs=[pl.BlockSpec(memory_space=pltpu.VMEM)] * 2,
        out_specs=pl.BlockSpec(memory_space=pltpu.VMEM),
        scratch_shapes=[
            pltpu.VMEM((NJ, NZ, CH, TOK), bf16),
            pltpu.VMEM((NY, NZ, TOK, SUB), bf16),
            pltpu.VMEM((4, 3, CH, SUB), f32),
            pltpu.VMEM((NJ, 2, HALF, SUB), bf16),
            pltpu.VMEM((NJ, 2, HALF, SUB), bf16),
            pltpu.VMEM((NJ, 2, CH, SUB), bf16),
            pltpu.VMEM((NJ, 2, CH, SUB), bf16),
            dma((NJ, 4, 2)),
            dma((NJ, 4, 2)),
            dma((NZ - 1,)),
            dma((NZ - 1,)),
            dma((NZ, 2, 2)),
            dma((NZ, 2, 2)),
            dma((NZ, 4)),
            dma((NZ, 4)),
            dma((NJ, 2, 2)),
            dma((NJ, 2, 2)),
        ],
        compiler_params=pltpu.CompilerParams(
            collective_id=0, has_side_effects=True, vmem_limit_bytes=48 * 2**20
        ),
        cost_estimate=pl.CostEstimate(
            flops=2 * 2 * FEAT * 1024 * 1024, bytes_accessed=3 * 2**20, transcendentals=0
        ),
        name="stats",
    )(quant_acts, full_acts)
    scale = 1.0 / (TOK * NX * NZ)
    return out[:FEAT] * scale, out[FEAT:] * scale


def solution(mesh):
    return jax.shard_map(
        local,
        mesh=mesh,
        in_specs=(P("col", "row"), P("col", "row")),
        out_specs=(P("row", "col"), P("row", "col")),
        check_vma=False,
    )
```

```python
import jax
import jax.numpy as jnp
from jax import lax
from jax.experimental import pallas as pl
from jax.experimental.pallas import tpu as pltpu
from jax.sharding import PartitionSpec as P

MESH = pl.DeviceIdType.MESH
NX, NY, NZ = 4, 4, 8
TOK, FEAT, SUB = 128, 1024, 256
CH = 128
NQ = FEAT // CH
NJ = 2 * NQ
HALF = CH // 2
PIECES = 1
ROWS = CH // PIECES
LAG = 2
XLAG = 2
YLAG = 3
PRE = 0
ORDER = (1, 7, 2, 6, 3, 5, 4)


def wrap(v, n):
    return lax.rem(v + n, n)


def kernel(q_hbm, f_hbm, o_ref, q_ref, f_ref, load, rows, cols, part, s1, r1, s2, r2,
           zsend, zrecv, asend, arecv, ysend, yrecv, ksend, krecv, xsend, xrecv):
    r, c = lax.axis_index("row"), lax.axis_index("col")
    y, k = lax.div(r, 2), lax.rem(r, 2)
    x, z = lax.div(c, NZ), lax.rem(c, NZ)
    xr, xl, xo = wrap(x + 1, NX), wrap(x - 1, NX), wrap(x + 2, NX)
    yr, yl, yo = wrap(y + 1, NY), wrap(y - 1, NY), wrap(y + 2, NY)
    zr, zl = wrap(z + 1, NZ), wrap(z - 1, NZ)
    owner = lax.div(z, 4) == k

    def dev(x, y, z, k):
        return (y * 2 + k, x * NZ + z)

    right, left = dev(x, y, zr, k), dev(x, y, zl, k)
    xright, xleft = dev(xr, y, z, k), dev(xl, y, z, k)
    up, down = dev(x, yr, z, k), dev(x, yl, z, k)
    other = dev(x, y, z, 1 - k)

    def remote(src, dst, send, recv, to):
        return pltpu.make_async_remote_copy(
            src_ref=src, dst_ref=dst, send_sem=send, recv_sem=recv, device_id=to, device_id_type=MESH
        )

    loads = [pltpu.make_async_copy(a, b, load.at[i]) for i, (a, b) in enumerate(((q_hbm, q_ref), (f_hbm, f_ref)))]
    for copy in loads:
        copy.start()

    barrier = pltpu.get_barrier_semaphore()
    for d in range(1, NZ):
        pl.semaphore_signal(barrier, inc=1, device_id=dev(x, y, wrap(z + d, NZ), k), device_id_type=MESH)
    for to in (xright, xleft, up, down, other):
        pl.semaphore_signal(barrier, inc=1, device_id=to, device_id_type=MESH)

    for copy in loads:
        copy.wait()
    for j in range(NQ):
        qj = q_ref[:, j * CH : (j + 1) * CH].astype(jnp.float32)
        fj = f_ref[:, j * CH : (j + 1) * CH].astype(jnp.float32)
        rows[j, z] = qj.T.astype(jnp.bfloat16)
        rows[NQ + j, z] = (fj - qj).astype(jnp.bfloat16).astype(jnp.float32).T.astype(jnp.bfloat16)

    pl.semaphore_wait(barrier, NZ - 1 + 5)

    def zref(p, at, s, way):
        j, start = lax.div(p, PIECES), lax.rem(p, PIECES) * ROWS
        if s == 3:
            return rows.at[j, at, pl.ds(pl.multiple_of(start + way * (ROWS // 2), ROWS // 2), ROWS // 2)]
        return rows.at[j, at, pl.ds(pl.multiple_of(start, ROWS), ROWS)]

    def zcopy(p, s, way):
        ref = zref(p, wrap(z - s, NZ) if way == 0 else lax.rem(z + s, NZ), s, way)
        return remote(ref, ref, zsend.at[p, s, way], zrecv.at[p, s, way], (right, left)[way])

    def zarrived(p, s, way):
        ref = zref(p, wrap(z - s - 1, NZ) if way == 0 else lax.rem(z + s + 1, NZ), s, way)
        remote(ref, ref, zsend.at[p, s, way], zrecv.at[p, s, way], (right, left)[way]).wait_recv()

    def zslot(t, guard=True):
        for s in range(4):
            p = t - s * LAG

            def go(p=p, s=s):
                for way in range(2):
                    if s > 0:
                        zarrived(p, s - 1, way)
                    zcopy(p, s, way).start()

            if guard:
                pl.when(jnp.logical_and(p >= 0, p < NJ * PIECES))(go)
            elif p >= 0:
                go()

    def acopy(d):
        to = wrap(z + d, NZ)
        src = q_ref.at[:, pl.ds(pl.multiple_of(lax.rem(to, 4) * SUB, SUB), SUB)]
        return remote(src, cols.at[y, z], asend.at[d - 1], arecv.at[d - 1], dev(x, y, to, k))

    for d in ORDER:
        pl.when(lax.div(wrap(z + d, NZ), 4) == k)(lambda d=d: acopy(d).start())

    @pl.when(owner)
    def _():
        cols[y, z] = q_ref[:, pl.ds(pl.multiple_of(lax.rem(z, 4) * SUB, SUB), SUB)]

    for t in range(PRE):
        zslot(t, False)

    def ycopy(b, i, s, way):
        if s == 0:
            ref = cols.at[y, b]
        else:
            ref = cols.at[(yl, yr)[way], b, pl.ds(way * 64, 64)]
        return remote(ref, ref, ysend.at[i, s, way], yrecv.at[i, s, way], (up, down)[way])

    def yarrived(b, i, s, way):
        if s == 0:
            ref = cols.at[(yl, yr)[way], b]
        else:
            ref = cols.at[yo, b, pl.ds(way * 64, 64)]
        remote(ref, ref, ysend.at[i, s, way], yrecv.at[i, s, way], (up, down)[way]).wait_recv()

    def kcopy(yb, b, i, n):
        ref = cols.at[yb, b]
        return remote(ref, ref, ksend.at[i, n], krecv.at[i, n], other)

    SRC = (0,) + ORDER

    def item(i):
        if i < NZ:
            d = SRC[i]
            b = wrap(z - d, NZ)
            if d:
                remote(cols.at[y, b], cols.at[y, b], asend.at[d - 1], arecv.at[d - 1], other).wait_recv()
            ycopy(b, i, 0, 0).start()
            ycopy(b, i, 0, 1).start()
            kcopy(y, b, i, 0).start()
        if 0 <= i - YLAG < NZ:
            n = i - YLAG
            b = wrap(z - SRC[n], NZ)
            for way in range(2):
                yarrived(b, n, 0, way)
                ycopy(b, n, 1, way).start()
                kcopy((yl, yr)[way], b, n, 1 + way).start()
        if 0 <= i - 2 * YLAG < NZ:
            n = i - 2 * YLAG
            b = wrap(z - SRC[n], NZ)
            for way in range(2):
                yarrived(b, n, 1, way)
            kcopy(yo, b, n, 3).start()

    FIRST = 4 * LAG // PIECES
    count, rest = NZ + 2 * YLAG, FIRST * PIECES - PRE
    for n in range(rest):
        @pl.when(owner)
        def _():
            for i in range(n * count // rest, (n + 1) * count // rest):
                item(i)

        zslot(PRE + n, False)

    @pl.when(jnp.logical_not(owner))
    def _():
        for i, d in enumerate(SRC):
            b = wrap(z - d, NZ)
            for n, yb in enumerate((y, yl, yr, yo)):
                kcopy(yb, b, i, n).wait_recv()

    def x1copy(j, way):
        return remote(s1.at[j, way], r1.at[j, way], xsend.at[j, 0, way], xrecv.at[j, 0, way], (xright, xleft)[way])

    def x2copy(j, way):
        return remote(s2.at[j, way], r2.at[j, way], xsend.at[j, 1, way], xrecv.at[j, 1, way], (xright, xleft)[way])

    def product(j):
        for n in range(PIECES):
            for way in range(2):
                zarrived(j * PIECES + n, 3, way)
        a = jnp.concatenate([rows[j, b] for b in range(NZ)], axis=1)

        def times(dest):
            b = cols[dest].reshape(NZ * TOK, SUB)
            return jnp.dot(a, b, preferred_element_type=jnp.float32)

        far = times(xo).astype(jnp.bfloat16)
        s1[j, 0] = far[:HALF]
        s1[j, 1] = far[HALF:]
        x1copy(j, 0).start()
        x1copy(j, 1).start()
        slot = lax.rem(j, 8)
        part[slot, 0] = times(xr)
        part[slot, 1] = times(xl)
        part[slot, 2] = times(x)

    def pass_on(j):
        slot = lax.rem(j, 8)
        x1copy(j, 0).wait_recv()
        s2[j, 0, :HALF] = (part[slot, 0, :HALF] + r1[j, 0].astype(jnp.float32)).astype(jnp.bfloat16)
        s2[j, 0, HALF:] = part[slot, 0, HALF:].astype(jnp.bfloat16)
        x2copy(j, 0).start()
        x1copy(j, 1).wait_recv()
        s2[j, 1, HALF:] = (part[slot, 1, HALF:] + r1[j, 1].astype(jnp.float32)).astype(jnp.bfloat16)
        s2[j, 1, :HALF] = part[slot, 1, :HALF].astype(jnp.bfloat16)
        x2copy(j, 1).start()

    def finish(j):
        slot = lax.rem(j, 8)
        x2copy(j, 0).wait_recv()
        x2copy(j, 1).wait_recv()
        total = part[slot, 2] + r2[j, 0].astype(jnp.float32) + r2[j, 1].astype(jnp.float32)
        o_ref[pl.ds(pl.multiple_of(j * CH, CH), CH), :] = total

    def slot(t, carry):
        for n in range(PIECES):
            zslot(t * PIECES + n)
        for lag, work in ((FIRST, product), (FIRST + XLAG, pass_on), (FIRST + 2 * XLAG, finish)):
            j = t - lag
            pl.when(jnp.logical_and(j >= 0, j < NJ))(lambda j=j, work=work: work(j))
        return carry

    lax.fori_loop(FIRST, NJ + FIRST + 2 * XLAG, slot, 0)

    def drain(j, carry):
        for way in range(2):
            for n in range(PIECES):
                for s in range(4):
                    zcopy(j * PIECES + n, s, way).wait_send()
            x1copy(j, way).wait_send()
            x2copy(j, way).wait_send()
        return carry

    lax.fori_loop(0, NJ, drain, 0)
    for d in ORDER:
        pl.when(lax.div(wrap(z + d, NZ), 4) == k)(lambda d=d: acopy(d).wait_send())

    @pl.when(owner)
    def _():
        for i, d in enumerate(SRC):
            b = wrap(z - d, NZ)
            for way in range(2):
                ycopy(b, i, 0, way).wait_send()
                ycopy(b, i, 1, way).wait_send()
            for n, yb in enumerate((y, yl, yr, yo)):
                kcopy(yb, b, i, n).wait_send()


def local(quant_acts, full_acts):
    bf16, f32, dma = jnp.bfloat16, jnp.float32, pltpu.SemaphoreType.DMA
    out = pl.pallas_call(
        kernel,
        out_shape=jax.ShapeDtypeStruct((2 * FEAT, SUB), f32),
        in_specs=[pl.BlockSpec(memory_space=pltpu.HBM)] * 2,
        out_specs=pl.BlockSpec(memory_space=pltpu.VMEM),
        scratch_shapes=[
            pltpu.VMEM((TOK, FEAT), bf16),
            pltpu.VMEM((TOK, FEAT), bf16),
            dma((2,)),
            pltpu.VMEM((NJ, NZ, CH, TOK), bf16),
            pltpu.VMEM((NY, NZ, TOK, SUB), bf16),
            pltpu.VMEM((8, 3, CH, SUB), f32),
            pltpu.VMEM((NJ, 2, HALF, SUB), bf16),
            pltpu.VMEM((NJ, 2, HALF, SUB), bf16),
            pltpu.VMEM((NJ, 2, CH, SUB), bf16),
            pltpu.VMEM((NJ, 2, CH, SUB), bf16),
            dma((NJ * PIECES, 4, 2)),
            dma((NJ * PIECES, 4, 2)),
            dma((NZ - 1,)),
            dma((NZ - 1,)),
            dma((NZ, 2, 2)),
            dma((NZ, 2, 2)),
            dma((NZ, 4)),
            dma((NZ, 4)),
            dma((NJ, 2, 2)),
            dma((NJ, 2, 2)),
        ],
        compiler_params=pltpu.CompilerParams(
            collective_id=0, has_side_effects=True, vmem_limit_bytes=48 * 2**20
        ),
        cost_estimate=pl.CostEstimate(
            flops=2 * 2 * FEAT * 1024 * 1024, bytes_accessed=3 * 2**20, transcendentals=0
        ),
        name="stats",
    )(*(pltpu.with_memory_space_constraint(a, pltpu.HBM) for a in (quant_acts, full_acts)))
    scale = 1.0 / (TOK * NX * NZ)
    return out[:FEAT] * scale, out[FEAT:] * scale


def solution(mesh):
    return jax.shard_map(
        local,
        mesh=mesh,
        in_specs=(P("col", "row"), P("col", "row")),
        out_specs=(P("row", "col"), P("row", "col")),
        check_vma=False,
    )
```

```python
import jax
import jax.numpy as jnp
from jax import lax
from jax.experimental import pallas as pl
from jax.experimental.pallas import tpu as pltpu
from jax.sharding import PartitionSpec as P

MESH = pl.DeviceIdType.MESH
NX, NY, NZ = 4, 4, 8
TOK, FEAT, SUB = 128, 1024, 256
CH = 128
NQ = FEAT // CH
NJ = 2 * NQ
HALF = CH // 2
AHEAD = (8, 6, 4, 2)
EARLY, LATE = (0, 1, 2, 3), ()
XLAG = 2
YLAG = 6
WAVES = ((1, 7, 2, 6, 3, 5, 4),)
WAVE_AT = (1,)
ORDER = sum(WAVES, ())


def wrap(v, n):
    return lax.rem(v + n, n)


def kernel(q_hbm, f_hbm, o_ref, q_ref, f_ref, load, rows, cols, part, s1, r1, s2, r2,
           zsend, zrecv, asend, arecv, ysend, yrecv, ksend, krecv, xsend, xrecv):
    r, c = lax.axis_index("row"), lax.axis_index("col")
    y, k = lax.div(r, 2), lax.rem(r, 2)
    x, z = lax.div(c, NZ), lax.rem(c, NZ)
    xr, xl, xo = wrap(x + 1, NX), wrap(x - 1, NX), wrap(x + 2, NX)
    yr, yl, yo = wrap(y + 1, NY), wrap(y - 1, NY), wrap(y + 2, NY)
    zr, zl = wrap(z + 1, NZ), wrap(z - 1, NZ)
    owner = lax.div(z, 4) == k

    def dev(x, y, z, k):
        return (y * 2 + k, x * NZ + z)

    right, left = dev(x, y, zr, k), dev(x, y, zl, k)
    xright, xleft = dev(xr, y, z, k), dev(xl, y, z, k)
    up, down = dev(x, yr, z, k), dev(x, yl, z, k)
    other = dev(x, y, z, 1 - k)

    def remote(src, dst, send, recv, to):
        return pltpu.make_async_remote_copy(
            src_ref=src, dst_ref=dst, send_sem=send, recv_sem=recv, device_id=to, device_id_type=MESH
        )

    loads = [pltpu.make_async_copy(a, b, load.at[i]) for i, (a, b) in enumerate(((q_hbm, q_ref), (f_hbm, f_ref)))]
    for copy in loads:
        copy.start()

    barrier = pltpu.get_barrier_semaphore()
    for d in range(1, NZ):
        pl.semaphore_signal(barrier, inc=1, device_id=dev(x, y, wrap(z + d, NZ), k), device_id_type=MESH)
    for to in (xright, xleft, up, down, other):
        pl.semaphore_signal(barrier, inc=1, device_id=to, device_id_type=MESH)

    for copy in loads:
        copy.wait()
    for j in range(NQ):
        qj = q_ref[:, j * CH : (j + 1) * CH].astype(jnp.float32)
        fj = f_ref[:, j * CH : (j + 1) * CH].astype(jnp.float32)
        rows[j, z] = qj.T.astype(jnp.bfloat16)
        rows[NQ + j, z] = (fj - qj).astype(jnp.bfloat16).astype(jnp.float32).T.astype(jnp.bfloat16)

    pl.semaphore_wait(barrier, NZ - 1 + 5)

    def zref(j, at, s, way):
        return rows.at[j, at, pl.ds(way * HALF, HALF)] if s == 3 else rows.at[j, at]

    def zcopy(j, s, way):
        ref = zref(j, wrap(z - s, NZ) if way == 0 else lax.rem(z + s, NZ), s, way)
        return remote(ref, ref, zsend.at[j, s, way], zrecv.at[j, s, way], (right, left)[way])

    def zarrived(j, s, way):
        ref = zref(j, wrap(z - s - 1, NZ) if way == 0 else lax.rem(z + s + 1, NZ), s, way)
        remote(ref, ref, zsend.at[j, s, way], zrecv.at[j, s, way], (right, left)[way]).wait_recv()

    def zhops(t, steps):
        for s in steps:
            j = t + AHEAD[s]

            def go(j=j, s=s):
                for way in range(2):
                    if s > 0:
                        zarrived(j, s - 1, way)
                    zcopy(j, s, way).start()

            if not isinstance(t, int):
                pl.when(j < NJ)(go)
            elif j >= 0:
                go()

    def acopy(d):
        to = wrap(z + d, NZ)
        src = q_ref.at[:, pl.ds(pl.multiple_of(lax.rem(to, 4) * SUB, SUB), SUB)]
        return remote(src, cols.at[y, z], asend.at[d - 1], arecv.at[d - 1], dev(x, y, to, k))

    def awave(n, what):
        for d in WAVES[n]:
            pl.when(lax.div(wrap(z + d, NZ), 4) == k)(lambda d=d: getattr(acopy(d), what)())

    awave(0, "start")

    @pl.when(owner)
    def _():
        cols[y, z] = q_ref[:, pl.ds(pl.multiple_of(lax.rem(z, 4) * SUB, SUB), SUB)]

    def ycopy(b, i, s, way):
        if s == 0:
            ref = cols.at[y, b]
        else:
            ref = cols.at[(yl, yr)[way], b, pl.ds(way * 64, 64)]
        return remote(ref, ref, ysend.at[i, s, way], yrecv.at[i, s, way], (up, down)[way])

    def yarrived(b, i, s, way):
        if s == 0:
            ref = cols.at[(yl, yr)[way], b]
        else:
            ref = cols.at[yo, b, pl.ds(way * 64, 64)]
        remote(ref, ref, ysend.at[i, s, way], yrecv.at[i, s, way], (up, down)[way]).wait_recv()

    def kcopy(yb, b, i, n):
        ref = cols.at[yb, b]
        return remote(ref, ref, ksend.at[i, n], krecv.at[i, n], other)

    SRC = (0,) + ORDER

    def item(i):
        if i < NZ:
            d = SRC[i]
            b = wrap(z - d, NZ)
            if d:
                remote(cols.at[y, b], cols.at[y, b], asend.at[d - 1], arecv.at[d - 1], other).wait_recv()
            ycopy(b, i, 0, 0).start()
            ycopy(b, i, 0, 1).start()
            kcopy(y, b, i, 0).start()
        if 0 <= i - YLAG < NZ:
            n = i - YLAG
            b = wrap(z - SRC[n], NZ)
            for way in range(2):
                yarrived(b, n, 0, way)
                ycopy(b, n, 1, way).start()
                kcopy((yl, yr)[way], b, n, 1 + way).start()
        if 0 <= i - 2 * YLAG < NZ:
            n = i - 2 * YLAG
            b = wrap(z - SRC[n], NZ)
            for way in range(2):
                yarrived(b, n, 1, way)
            kcopy(yo, b, n, 3).start()

    count, parts = NZ + 2 * YLAG, 2 * AHEAD[0]
    for n in range(parts):
        for wave in range(1, len(WAVES)):
            if WAVE_AT[wave] == n:
                awave(wave - 1, "wait_send")
                awave(wave, "start")

        @pl.when(owner)
        def _():
            for i in range(n * count // parts, (n + 1) * count // parts):
                item(i)

        zhops(n // 2 - AHEAD[0], (EARLY, LATE)[n % 2])

    @pl.when(jnp.logical_not(owner))
    def _():
        for i, d in enumerate(SRC):
            b = wrap(z - d, NZ)
            for n, yb in enumerate((y, yl, yr, yo)):
                kcopy(yb, b, i, n).wait_recv()

    def x1copy(j, way):
        return remote(s1.at[j, way], r1.at[j, way], xsend.at[j, 0, way], xrecv.at[j, 0, way], (xright, xleft)[way])

    def x2copy(j, way):
        return remote(s2.at[j, way], r2.at[j, way], xsend.at[j, 1, way], xrecv.at[j, 1, way], (xright, xleft)[way])

    def product(j):
        for way in range(2):
            zarrived(j, 3, way)
        a = jnp.concatenate([rows[j, b] for b in range(NZ)], axis=1)

        def times(dest):
            b = cols[dest].reshape(NZ * TOK, SUB)
            return jnp.dot(a, b, preferred_element_type=jnp.float32)

        far = times(xo).astype(jnp.bfloat16)
        s1[j, 0] = far[:HALF]
        s1[j, 1] = far[HALF:]
        x1copy(j, 0).start()
        x1copy(j, 1).start()
        slot = lax.rem(j, 8)
        part[slot, 0] = times(xr)
        part[slot, 1] = times(xl)
        part[slot, 2] = times(x)

    def pass_on(j):
        slot = lax.rem(j, 8)
        x1copy(j, 0).wait_recv()
        s2[j, 0, :HALF] = (part[slot, 0, :HALF] + r1[j, 0].astype(jnp.float32)).astype(jnp.bfloat16)
        s2[j, 0, HALF:] = part[slot, 0, HALF:].astype(jnp.bfloat16)
        x2copy(j, 0).start()
        x1copy(j, 1).wait_recv()
        s2[j, 1, HALF:] = (part[slot, 1, HALF:] + r1[j, 1].astype(jnp.float32)).astype(jnp.bfloat16)
        s2[j, 1, :HALF] = part[slot, 1, :HALF].astype(jnp.bfloat16)
        x2copy(j, 1).start()

    def finish(j):
        slot = lax.rem(j, 8)
        x2copy(j, 0).wait_recv()
        x2copy(j, 1).wait_recv()
        total = part[slot, 2] + r2[j, 0].astype(jnp.float32) + r2[j, 1].astype(jnp.float32)
        o_ref[pl.ds(pl.multiple_of(j * CH, CH), CH), :] = total

    def slot(t, carry):
        zhops(t, EARLY)
        pl.when(t < NJ)(lambda: product(t))
        zhops(t, LATE)
        for lag, work in ((XLAG, pass_on), (2 * XLAG, finish)):
            j = t - lag
            pl.when(jnp.logical_and(j >= 0, j < NJ))(lambda j=j, work=work: work(j))
        return carry

    lax.fori_loop(0, NJ + 2 * XLAG, slot, 0)

    def drain(j, carry):
        for way in range(2):
            for s in range(4):
                zcopy(j, s, way).wait_send()
            x1copy(j, way).wait_send()
            x2copy(j, way).wait_send()
        return carry

    lax.fori_loop(0, NJ, drain, 0)
    awave(len(WAVES) - 1, "wait_send")

    @pl.when(owner)
    def _():
        for i, d in enumerate(SRC):
            b = wrap(z - d, NZ)
            for way in range(2):
                ycopy(b, i, 0, way).wait_send()
                ycopy(b, i, 1, way).wait_send()
            for n, yb in enumerate((y, yl, yr, yo)):
                kcopy(yb, b, i, n).wait_send()


def local(quant_acts, full_acts):
    bf16, f32, dma = jnp.bfloat16, jnp.float32, pltpu.SemaphoreType.DMA
    out = pl.pallas_call(
        kernel,
        out_shape=jax.ShapeDtypeStruct((2 * FEAT, SUB), f32),
        in_specs=[pl.BlockSpec(memory_space=pltpu.HBM)] * 2,
        out_specs=pl.BlockSpec(memory_space=pltpu.VMEM),
        scratch_shapes=[
            pltpu.VMEM((TOK, FEAT), bf16),
            pltpu.VMEM((TOK, FEAT), bf16),
            dma((2,)),
            pltpu.VMEM((NJ, NZ, CH, TOK), bf16),
            pltpu.VMEM((NY, NZ, TOK, SUB), bf16),
            pltpu.VMEM((8, 3, CH, SUB), f32),
            pltpu.VMEM((NJ, 2, HALF, SUB), bf16),
            pltpu.VMEM((NJ, 2, HALF, SUB), bf16),
            pltpu.VMEM((NJ, 2, CH, SUB), bf16),
            pltpu.VMEM((NJ, 2, CH, SUB), bf16),
            dma((NJ, 4, 2)),
            dma((NJ, 4, 2)),
            dma((NZ - 1,)),
            dma((NZ - 1,)),
            dma((NZ, 2, 2)),
            dma((NZ, 2, 2)),
            dma((NZ, 4)),
            dma((NZ, 4)),
            dma((NJ, 2, 2)),
            dma((NJ, 2, 2)),
        ],
        compiler_params=pltpu.CompilerParams(
            collective_id=0, has_side_effects=True, vmem_limit_bytes=48 * 2**20
        ),
        cost_estimate=pl.CostEstimate(
            flops=2 * 2 * FEAT * 1024 * 1024, bytes_accessed=3 * 2**20, transcendentals=0
        ),
        name="stats",
    )(*(pltpu.with_memory_space_constraint(a, pltpu.HBM) for a in (quant_acts, full_acts)))
    scale = 1.0 / (TOK * NX * NZ)
    return out[:FEAT] * scale, out[FEAT:] * scale


def solution(mesh):
    return jax.shard_map(
        local,
        mesh=mesh,
        in_specs=(P("col", "row"), P("col", "row")),
        out_specs=(P("row", "col"), P("row", "col")),
        check_vma=False,
    )
```

```python
import jax
import jax.numpy as jnp
from jax import lax
from jax.experimental import pallas as pl
from jax.experimental.pallas import tpu as pltpu
from jax.sharding import PartitionSpec as P

MESH = pl.DeviceIdType.MESH
NX, NY, NZ = 4, 4, 8
TOK, FEAT, SUB = 128, 1024, 256
CH = 128
NQ = FEAT // CH
NJ = 2 * NQ
HALF = CH // 2
AHEAD = (8, 6, 4, 2)
EARLY, LATE = (0, 1, 2, 3), ()
XLAG = 2
YLAG = 6
WAVES = ((1, 7, 2, 6, 3, 5, 4),)
WAVE_AT = (1,)
ORDER = sum(WAVES, ())


def wrap(v, n):
    return lax.rem(v + n, n)


def kernel(q_hbm, f_hbm, o_ref, q_ref, f_ref, load, rows, cols, part, s1, r1, s2, r2,
           zsend, zrecv, asend, arecv, ysend, yrecv, ksend, krecv, xsend, xrecv):
    r, c = lax.axis_index("row"), lax.axis_index("col")
    y, k = lax.div(r, 2), lax.rem(r, 2)
    x, z = lax.div(c, NZ), lax.rem(c, NZ)
    xr, xl, xo = wrap(x + 1, NX), wrap(x - 1, NX), wrap(x + 2, NX)
    yr, yl, yo = wrap(y + 1, NY), wrap(y - 1, NY), wrap(y + 2, NY)
    zr, zl = wrap(z + 1, NZ), wrap(z - 1, NZ)
    owner = lax.div(z, 4) == k

    def dev(x, y, z, k):
        return (y * 2 + k, x * NZ + z)

    right, left = dev(x, y, zr, k), dev(x, y, zl, k)
    xright, xleft = dev(xr, y, z, k), dev(xl, y, z, k)
    up, down = dev(x, yr, z, k), dev(x, yl, z, k)
    other = dev(x, y, z, 1 - k)

    def remote(src, dst, send, recv, to):
        return pltpu.make_async_remote_copy(
            src_ref=src, dst_ref=dst, send_sem=send, recv_sem=recv, device_id=to, device_id_type=MESH
        )

    loads = [pltpu.make_async_copy(a, b, load.at[i]) for i, (a, b) in enumerate(((q_hbm, q_ref), (f_hbm, f_ref)))]
    for copy in loads:
        copy.start()

    barrier = pltpu.get_barrier_semaphore()
    for d in range(1, NZ):
        pl.semaphore_signal(barrier, inc=1, device_id=dev(x, y, wrap(z + d, NZ), k), device_id_type=MESH)
    for to in (xright, xleft, up, down, other):
        pl.semaphore_signal(barrier, inc=1, device_id=to, device_id_type=MESH)

    loads[0].wait()
    for j in range(NQ):
        rows[j, z] = q_ref[:, j * CH : (j + 1) * CH].astype(jnp.float32).T.astype(jnp.bfloat16)

    pl.semaphore_wait(barrier, NZ - 1 + 5)

    def zref(j, at, s, way):
        return rows.at[j, at, pl.ds(way * HALF, HALF)] if s == 3 else rows.at[j, at]

    def zcopy(j, s, way):
        ref = zref(j, wrap(z - s, NZ) if way == 0 else lax.rem(z + s, NZ), s, way)
        return remote(ref, ref, zsend.at[j, s, way], zrecv.at[j, s, way], (right, left)[way])

    def zarrived(j, s, way):
        ref = zref(j, wrap(z - s - 1, NZ) if way == 0 else lax.rem(z + s + 1, NZ), s, way)
        remote(ref, ref, zsend.at[j, s, way], zrecv.at[j, s, way], (right, left)[way]).wait_recv()

    def zhops(t, steps):
        for s in steps:
            j = t + AHEAD[s]

            def go(j=j, s=s):
                for way in range(2):
                    if s > 0:
                        zarrived(j, s - 1, way)
                    zcopy(j, s, way).start()

            if not isinstance(t, int):
                pl.when(j < NJ)(go)
            elif j >= 0:
                go()

    def acopy(d):
        to = wrap(z + d, NZ)
        src = q_ref.at[:, pl.ds(pl.multiple_of(lax.rem(to, 4) * SUB, SUB), SUB)]
        return remote(src, cols.at[y, z], asend.at[d - 1], arecv.at[d - 1], dev(x, y, to, k))

    def awave(n, what):
        for d in WAVES[n]:
            pl.when(lax.div(wrap(z + d, NZ), 4) == k)(lambda d=d: getattr(acopy(d), what)())

    awave(0, "start")
    loads[1].wait()
    for j in range(NQ):
        qj = q_ref[:, j * CH : (j + 1) * CH].astype(jnp.float32)
        fj = f_ref[:, j * CH : (j + 1) * CH].astype(jnp.float32)
        rows[NQ + j, z] = (fj - qj).astype(jnp.bfloat16).astype(jnp.float32).T.astype(jnp.bfloat16)

    @pl.when(owner)
    def _():
        cols[y, z] = q_ref[:, pl.ds(pl.multiple_of(lax.rem(z, 4) * SUB, SUB), SUB)]

    def ycopy(b, i, s, way):
        if s == 0:
            ref = cols.at[y, b]
        else:
            ref = cols.at[(yl, yr)[way], b, pl.ds(way * 64, 64)]
        return remote(ref, ref, ysend.at[i, s, way], yrecv.at[i, s, way], (up, down)[way])

    def yarrived(b, i, s, way):
        if s == 0:
            ref = cols.at[(yl, yr)[way], b]
        else:
            ref = cols.at[yo, b, pl.ds(way * 64, 64)]
        remote(ref, ref, ysend.at[i, s, way], yrecv.at[i, s, way], (up, down)[way]).wait_recv()

    def kcopy(yb, b, i, n):
        ref = cols.at[yb, b]
        return remote(ref, ref, ksend.at[i, n], krecv.at[i, n], other)

    SRC = (0,) + ORDER

    def item(i):
        if i < NZ:
            d = SRC[i]
            b = wrap(z - d, NZ)
            if d:
                remote(cols.at[y, b], cols.at[y, b], asend.at[d - 1], arecv.at[d - 1], other).wait_recv()
            ycopy(b, i, 0, 0).start()
            ycopy(b, i, 0, 1).start()
            kcopy(y, b, i, 0).start()
        if 0 <= i - YLAG < NZ:
            n = i - YLAG
            b = wrap(z - SRC[n], NZ)
            for way in range(2):
                yarrived(b, n, 0, way)
                ycopy(b, n, 1, way).start()
                kcopy((yl, yr)[way], b, n, 1 + way).start()
        if 0 <= i - 2 * YLAG < NZ:
            n = i - 2 * YLAG
            b = wrap(z - SRC[n], NZ)
            for way in range(2):
                yarrived(b, n, 1, way)
            kcopy(yo, b, n, 3).start()

    count, parts = NZ + 2 * YLAG, 2 * AHEAD[0]
    for n in range(parts):
        for wave in range(1, len(WAVES)):
            if WAVE_AT[wave] == n:
                awave(wave - 1, "wait_send")
                awave(wave, "start")

        @pl.when(owner)
        def _():
            for i in range(n * count // parts, (n + 1) * count // parts):
                item(i)

        zhops(n // 2 - AHEAD[0], (EARLY, LATE)[n % 2])

    @pl.when(jnp.logical_not(owner))
    def _():
        for i, d in enumerate(SRC):
            b = wrap(z - d, NZ)
            for n, yb in enumerate((y, yl, yr, yo)):
                kcopy(yb, b, i, n).wait_recv()

    def x1copy(j, way):
        return remote(s1.at[j, way], r1.at[j, way], xsend.at[j, 0, way], xrecv.at[j, 0, way], (xright, xleft)[way])

    def x2copy(j, way):
        return remote(s2.at[j, way], r2.at[j, way], xsend.at[j, 1, way], xrecv.at[j, 1, way], (xright, xleft)[way])

    def product(j):
        for way in range(2):
            zarrived(j, 3, way)
        a = jnp.concatenate([rows[j, b] for b in range(NZ)], axis=1)

        def times(dest):
            b = cols[dest].reshape(NZ * TOK, SUB)
            return jnp.dot(a, b, preferred_element_type=jnp.float32)

        far = times(xo).astype(jnp.bfloat16)
        s1[j, 0] = far[:HALF]
        s1[j, 1] = far[HALF:]
        x1copy(j, 0).start()
        x1copy(j, 1).start()
        slot = lax.rem(j, 8)
        part[slot, 0] = times(xr)
        part[slot, 1] = times(xl)
        part[slot, 2] = times(x)

    def pass_on(j):
        slot = lax.rem(j, 8)
        x1copy(j, 0).wait_recv()
        s2[j, 0, :HALF] = (part[slot, 0, :HALF] + r1[j, 0].astype(jnp.float32)).astype(jnp.bfloat16)
        s2[j, 0, HALF:] = part[slot, 0, HALF:].astype(jnp.bfloat16)
        x2copy(j, 0).start()
        x1copy(j, 1).wait_recv()
        s2[j, 1, HALF:] = (part[slot, 1, HALF:] + r1[j, 1].astype(jnp.float32)).astype(jnp.bfloat16)
        s2[j, 1, :HALF] = part[slot, 1, :HALF].astype(jnp.bfloat16)
        x2copy(j, 1).start()

    def finish(j):
        slot = lax.rem(j, 8)
        x2copy(j, 0).wait_recv()
        x2copy(j, 1).wait_recv()
        total = part[slot, 2] + r2[j, 0].astype(jnp.float32) + r2[j, 1].astype(jnp.float32)
        o_ref[pl.ds(pl.multiple_of(j * CH, CH), CH), :] = total

    def slot(t, carry):
        zhops(t, EARLY)
        pl.when(t < NJ)(lambda: product(t))
        zhops(t, LATE)
        for lag, work in ((XLAG, pass_on), (2 * XLAG, finish)):
            j = t - lag
            pl.when(jnp.logical_and(j >= 0, j < NJ))(lambda j=j, work=work: work(j))
        return carry

    lax.fori_loop(0, NJ + 2 * XLAG, slot, 0)

    def drain(j, carry):
        for way in range(2):
            for s in range(4):
                zcopy(j, s, way).wait_send()
            x1copy(j, way).wait_send()
            x2copy(j, way).wait_send()
        return carry

    lax.fori_loop(0, NJ, drain, 0)
    awave(len(WAVES) - 1, "wait_send")

    @pl.when(owner)
    def _():
        for i, d in enumerate(SRC):
            b = wrap(z - d, NZ)
            for way in range(2):
                ycopy(b, i, 0, way).wait_send()
                ycopy(b, i, 1, way).wait_send()
            for n, yb in enumerate((y, yl, yr, yo)):
                kcopy(yb, b, i, n).wait_send()


def local(quant_acts, full_acts):
    bf16, f32, dma = jnp.bfloat16, jnp.float32, pltpu.SemaphoreType.DMA
    out = pl.pallas_call(
        kernel,
        out_shape=jax.ShapeDtypeStruct((2 * FEAT, SUB), f32),
        in_specs=[pl.BlockSpec(memory_space=pltpu.HBM)] * 2,
        out_specs=pl.BlockSpec(memory_space=pltpu.VMEM),
        scratch_shapes=[
            pltpu.VMEM((TOK, FEAT), bf16),
            pltpu.VMEM((TOK, FEAT), bf16),
            dma((2,)),
            pltpu.VMEM((NJ, NZ, CH, TOK), bf16),
            pltpu.VMEM((NY, NZ, TOK, SUB), bf16),
            pltpu.VMEM((8, 3, CH, SUB), f32),
            pltpu.VMEM((NJ, 2, HALF, SUB), bf16),
            pltpu.VMEM((NJ, 2, HALF, SUB), bf16),
            pltpu.VMEM((NJ, 2, CH, SUB), bf16),
            pltpu.VMEM((NJ, 2, CH, SUB), bf16),
            dma((NJ, 4, 2)),
            dma((NJ, 4, 2)),
            dma((NZ - 1,)),
            dma((NZ - 1,)),
            dma((NZ, 2, 2)),
            dma((NZ, 2, 2)),
            dma((NZ, 4)),
            dma((NZ, 4)),
            dma((NJ, 2, 2)),
            dma((NJ, 2, 2)),
        ],
        compiler_params=pltpu.CompilerParams(
            collective_id=0, has_side_effects=True, vmem_limit_bytes=48 * 2**20
        ),
        cost_estimate=pl.CostEstimate(
            flops=2 * 2 * FEAT * 1024 * 1024, bytes_accessed=3 * 2**20, transcendentals=0
        ),
        name="stats",
    )(*(pltpu.with_memory_space_constraint(a, pltpu.HBM) for a in (quant_acts, full_acts)))
    scale = 1.0 / (TOK * NX * NZ)
    return out[:FEAT] * scale, out[FEAT:] * scale


def solution(mesh):
    return jax.shard_map(
        local,
        mesh=mesh,
        in_specs=(P("col", "row"), P("col", "row")),
        out_specs=(P("row", "col"), P("row", "col")),
        check_vma=False,
    )
```
